32 devices in a mesh: wave: 8 (over z, y), lon: 4 (over x, core).
Axes of the slice: x: 2, y: 2, z: 4, core: 2. Of those that a mesh axis runs over, the one named last changes fastest.
Arguments:
- spectra: bfloat16 [640, 2, 3, 8, 1281], P('wave', None, None, 'lon'), may hold values from -6 to 6
- legendre: bfloat16 [640, 8, 1281], P('wave'), may hold values from -0.0034179688 to 0.0034179688
- pair_waves: int32 [640], replicated, may hold values from 0 to 639, each once
- row_lengths: int32 [8], P('wave'), may hold values from 1280 to 5120, as said below
- departure: int32 [8, 8, 4, 1280], P('wave', None, 'lon'), may hold values from -7 to 6
- weights: bfloat16 [4, 8, 8, 4, 1280], P(None, 'wave', None, 'lon'), may hold values from -0.29882812 to 0.796875
Outputs:
- departed: bfloat16 [3, 8, 8, 4, 1280], P(None, 'wave', None, 'lon')
The draws below stay inside these ranges and needn't reach their ends.
Inputs may be any that keep to these rules, and one draw needn't show every extreme that they name: Pair slot p holds wavenumbers pair_waves[p] and 1279 - pair_waves[p]; every value appears once. `row_lengths`: every row length is a multiple of 8.
All inputs are finite; a program needn't handle non-finite values.
Results may differ from the reference program's by a relative error of at most 0.0059.
Values may be sent and summed in bfloat16 or wider, within the bound.
A program may use at most 192 MiB of HBM per device.

```python
import math
import jax
import jax.numpy as jnp
from jax import lax

TRUNC = 1279
LMAX = 5120
HALO = 8
PAIRS = 640
NPK = 1281
LATS = 8
LEV = 8
SEGS = 4
SEG = 1280


def draw_row_lengths(key, part):
    key_one, key_two = jax.random.split(key)
    counts = jax.random.randint(key_one, (LATS,), LMAX // 32, LMAX // 8 + 1)
    lengths = 8 * counts
    places = jax.random.permutation(key_two, LATS)
    lengths = lengths.at[places[0]].set(LMAX)
    lengths = lengths.at[places[1]].set(LMAX // 4)
    return lengths.astype(jnp.int32)


def touch_ends(entries, own_key, least, high):
    index_at = [jax.random.randint(jax.random.fold_in(own_key, axis), (), 0, length) for axis, length in enumerate(entries.shape)]
    main_axis = entries.shape.index(max(entries.shape))
    beside = index_at[:main_axis] + [(index_at[main_axis] + 1) % entries.shape[main_axis]] + index_at[main_axis + 1:]
    return entries.at[tuple(index_at)].set(least).at[tuple(beside)].set(high)


def levels(key, extent, shards, least, high):
    level = 1.0
    for dim, blocks in shards:
        heights = jax.random.uniform(jax.random.fold_in(jax.random.fold_in(key, 6), dim), (blocks,), jnp.float32, least / len(shards), high / len(shards))
        level = level * jnp.repeat(jnp.exp(heights), extent[dim] // blocks).reshape((-1,) + (1,) * (len(extent) - 1 - dim))
    return level


def scatter_about(key, dims, spread, most, pieces=(), kind=jnp.bfloat16):
    gain = levels(key, dims, pieces, -0.22, 0.18) if pieces else 1.0
    result = jax.random.normal(key, dims, jnp.float32) * spread * gain
    return jnp.minimum(jnp.maximum(result, -most), most).astype(kind)


def setup_inputs(seed: int = 0) -> dict:
    splits = jax.random.split(jax.random.key(seed), 7)
    return {
        "spectra": scatter_about(splits[0], (PAIRS, 2, 3, LEV, NPK), 1.0, 6.0, ((0, 8), (3, 4))),
        "legendre": scatter_about(splits[1], (PAIRS, LATS, NPK), (2 * NPK * (TRUNC + 1)) ** -0.5, 0.0034179688, ((0, 8),)),
        "pair_waves": jax.random.permutation(splits[2], PAIRS).astype(jnp.int32),
        "row_lengths": draw_row_lengths(jax.random.fold_in(splits[6], 71), 0),
        "departure": touch_ends(jax.random.randint(splits[4], (LATS, LEV, SEGS, SEG), 1 - HALO, HALO - 1), jax.random.fold_in(splits[4], 1), 1 - HALO, (HALO - 1) - 1).astype(jnp.int32),
        "weights": jnp.clip(-0.29882812 + 1.0957031 * jax.random.uniform(splits[5], (4, LATS, LEV, SEGS, SEG), jnp.float32) ** levels(splits[5], (4, LATS, LEV, SEGS, SEG), ((1, 8), (3, 4)), -0.2, 0.2), -0.29882812, 0.796875).astype(jnp.bfloat16),
    }


def build_table(wavenumbers, lengths, segment, seg_width, seg_count):
    seg_share = lengths // seg_count
    slot_index = jnp.arange(seg_width, dtype=jnp.int32)
    longitude = segment * seg_share[:, None] + slot_index[None, :]
    inside = slot_index[None, :] < seg_share[:, None]
    row_len = lengths[:, None, None, None]
    wave_grid = wavenumbers[None, :, :, None]
    residue = (wave_grid * longitude[:, None, None, :]) % row_len
    angles = (2.0 * math.pi) * residue.astype(jnp.float32) / row_len.astype(jnp.float32)
    highest = row_len // 2 - 1
    factor = jnp.where(wave_grid == 0, 1.0, jnp.where(wave_grid <= highest, 2.0, 0.0)).astype(jnp.float32)
    factor = jnp.where(inside[:, None, None, :], factor, jnp.zeros_like(factor))
    cosine = (factor * jnp.cos(angles)).astype(jnp.bfloat16)
    sines = (-factor * jnp.sin(angles)).astype(jnp.bfloat16)
    return jnp.stack([cosine, sines], axis=1)


def reference(spectra, legendre, pair_waves, row_lengths, departure, weights):
    packed = TRUNC + 2

    def one_pair(items):
        leg_rows, coefficients, wave_first = items
        keeper = jnp.arange(packed, dtype=jnp.int32) < (TRUNC + 1 - wave_first)
        flat = coefficients.reshape(6 * LEV, packed)
        part_one = jnp.where(keeper[None, :], flat, jnp.zeros_like(flat))
        part_two = jnp.where(keeper[None, :], jnp.zeros_like(flat), flat)
        first_sum = jnp.dot(part_one, leg_rows.T, preferred_element_type=jnp.float32)
        second_sum = jnp.dot(part_two, leg_rows.T, preferred_element_type=jnp.float32)
        return jnp.stack([first_sum, second_sum]).astype(jnp.bfloat16)

    fourier = lax.map(one_pair, (legendre, spectra, pair_waves))
    fourier = fourier.reshape(PAIRS, 2, 2, 3, LEV, LATS).astype(jnp.float32)
    wavenumbers = jnp.stack([pair_waves, TRUNC - pair_waves], axis=1)
    blocks = []
    for segment in range(SEGS):
        table = build_table(wavenumbers, row_lengths, segment, SEG, SEGS).astype(jnp.float32)
        product = jnp.einsum("pwrfvj,jrpwk->fjvk", fourier, table, precision=lax.Precision.HIGHEST)
        blocks.append(product.astype(jnp.bfloat16))
    grid = jnp.stack(blocks, axis=3)
    seg_share = row_lengths // SEGS
    flat_grid = grid.reshape(3, LATS, LEV, SEGS * SEG)
    segment_index = jnp.arange(SEGS, dtype=jnp.int32)
    slot_index = jnp.arange(SEG, dtype=jnp.int32)
    longitude = segment_index[None, :, None] * seg_share[:, None, None] + slot_index[None, None, :]
    base_point = longitude[:, None, :, :] + departure
    share_wide = seg_share[:, None, None, None]
    length_wide = row_lengths[:, None, None, None]
    total = jnp.zeros((3, LATS, LEV, SEGS, SEG), jnp.float32)
    for corner in range(4):
        cell = (base_point + (corner - 1)) % length_wide
        column = (cell // share_wide) * SEG + cell % share_wide
        column = column.reshape(LATS, LEV, SEGS * SEG)
        picked = jnp.take_along_axis(flat_grid, jnp.broadcast_to(column[None], flat_grid.shape), axis=3)
        picked = picked.reshape(3, LATS, LEV, SEGS, SEG)
        total = total + weights[corner][None].astype(jnp.float32) * picked.astype(jnp.float32)
    inside = slot_index[None, :] < seg_share[:, None]
    total = jnp.where(inside[None, :, None, None, :], total, jnp.zeros_like(total))
    return total.astype(jnp.bfloat16)
```

```python
import functools
import math

import jax
import jax.numpy as jnp
from jax import lax
from jax.experimental import pallas as pl
from jax.experimental.pallas import tpu as pltpu
from jax.sharding import PartitionSpec as P

TRUNC = 1279
HALO = 8
LANES = 128
SHIFTS = 2 * HALO + 1
SPAN = LANES + 2 * HALO


def unit_circle(waves, points, length, inverse):
    product = waves * points
    turns = jnp.floor(product * inverse + 0.5)
    half = (product - turns * length) * (inverse * math.pi)
    sq = half * half
    sine, cosine = 0.0, 0.0
    for k in range(7, -1, -1):
        sine = sine * sq + (-1.0) ** k / math.factorial(2 * k + 1)
        cosine = cosine * sq + (-1.0) ** k / math.factorial(2 * k)
    sine = sine * half
    return 1.0 - 2.0 * sine * sine, 2.0 * sine * cosine


def make_tables(seg_count, pairs_ref, length, table_ref, start_cos, start_sin):
    first = pairs_ref[...].astype(jnp.float32)
    waves = jnp.concatenate([first, TRUNC - first], axis=1)
    modes = waves.shape[1]
    length_f = length.astype(jnp.float32)
    inverse = 1.0 / jnp.full((1, 1), length_f, jnp.float32)
    fine_at = lax.broadcasted_iota(jnp.int32, (16, modes), 0).astype(jnp.float32)
    cos_f, sin_f = unit_circle(waves, fine_at, length_f, inverse)
    cos_c, sin_c = unit_circle(waves, fine_at * 16.0, length_f, inverse)
    for a in range(SPAN // 16):
        ca, sa = cos_c[a : a + 1], sin_c[a : a + 1]
        rows = slice(16 * a, 16 * a + 16)
        table_ref[rows, :modes] = (cos_f * ca - sin_f * sa).astype(jnp.bfloat16)
        table_ref[rows, modes:] = (-(sin_f * ca + cos_f * sa)).astype(jnp.bfloat16)
    share = length // seg_count
    start = (lax.axis_index("lon") * share - HALO).astype(jnp.float32)
    cos_s, sin_s = unit_circle(waves, fine_at * float(LANES) + start, length_f, inverse)
    highest = (length // 2 - 1).astype(jnp.float32)
    factor = jnp.where(waves == 0.0, 1.0, jnp.where(waves <= highest, 2.0, 0.0))
    start_cos[...] = cos_s * factor
    start_sin[...] = sin_s * factor


def synthesize(real, imag, blocks, table_ref, start_cos, start_sin, lhs_ref, grid_ref):
    rows, modes = real.shape
    for h in range(blocks):
        c, s = start_cos[h : h + 1], start_sin[h : h + 1]
        at = slice(h * rows, (h + 1) * rows)
        lhs_ref[at, :modes] = real * c - imag * s
        lhs_ref[at, modes:] = real * s + imag * c
    grid_ref[:, :SPAN] = lax.dot_general(
        lhs_ref[...].astype(jnp.bfloat16),
        table_ref[...],
        (((1,), (1,)), ((), ())),
        preferred_element_type=jnp.float32,
    )


def depart(share, blocks, levels, departure_ref, weights_ref, grid_ref, out_ref):
    rows = 3 * levels
    for h in range(blocks):
        lanes = slice(h * LANES, (h + 1) * LANES)
        cell = departure_ref[:, lanes]
        factors = [weights_ref[c, :, lanes].astype(jnp.float32) for c in range(4)]
        totals = [jnp.zeros((levels, LANES), jnp.float32)] * 3
        for s in range(SHIFTS):
            weight = jnp.zeros((levels, LANES), jnp.float32)
            for c in range(4):
                if 1 - HALO <= s - 7 - c <= HALO - 2:
                    weight = weight + jnp.where(cell == s - 7 - c, factors[c], 0.0)
            moved = grid_ref[h * rows : (h + 1) * rows, s : s + LANES]
            for f in range(3):
                totals[f] = totals[f] + weight * moved[f * levels : (f + 1) * levels]
        slot = h * LANES + lax.broadcasted_iota(jnp.int32, (levels, LANES), 1)
        for f in range(3):
            kept = jnp.where(slot < share, totals[f], 0.0)
            out_ref[f, :, lanes] = kept.astype(jnp.bfloat16)


def row_kernel(
    seg_count, length_ref, pairs_ref, fourier_ref, departure_ref, weights_ref, out_ref,
    table_ref, start_cos, start_sin, lhs_ref, grid_ref,
):
    length = length_ref[0]
    levels, width = departure_ref.shape
    blocks = width // LANES
    make_tables(seg_count, pairs_ref, length, table_ref, start_cos, start_sin)
    real = fourier_ref[0].astype(jnp.float32)
    imag = fourier_ref[1].astype(jnp.float32)
    synthesize(real, imag, blocks, table_ref, start_cos, start_sin, lhs_ref, grid_ref)
    depart(length // seg_count, blocks, levels, departure_ref, weights_ref, grid_ref, out_ref)


def local(spectra, legendre, pair_waves, row_lengths, departure, weights):
    pair_dev = spectra.shape[0]
    level_dev = spectra.shape[3]
    packed = spectra.shape[4]
    row_total = legendre.shape[1]
    pairs = pair_waves.shape[0]
    levels, width = departure.shape[1], departure.shape[3]
    seg_count = lax.axis_size("lon")
    columns = 6 * level_dev
    start_pair = lax.axis_index("wave") * pair_dev
    own_waves = lax.dynamic_slice_in_dim(pair_waves, start_pair, pair_dev)
    flat_spec = spectra.reshape(pair_dev, columns, packed)
    keeper = jnp.arange(packed, dtype=jnp.int32)[None, :] < (TRUNC + 1 - own_waves)[:, None]
    keeper = keeper[:, None, :]
    blank = jnp.zeros_like(flat_spec)
    doubled = jnp.stack(
        [jnp.where(keeper, flat_spec, blank), jnp.where(keeper, blank, flat_spec)], axis=1
    )
    fourier = jnp.einsum("pwcn,pln->pwcl", doubled, legendre, preferred_element_type=jnp.float32)
    fourier = fourier.astype(jnp.bfloat16).reshape(pair_dev, 2, 2, 3, level_dev, row_total)
    by_rows = lax.all_to_all(fourier, "wave", split_axis=5, concat_axis=0, tiled=True)
    whole = lax.all_gather(by_rows, "lon", axis=4, tiled=True)
    whole = jnp.transpose(whole[..., 0], (2, 3, 4, 1, 0)).reshape(2, 3 * levels, 2 * pairs)
    blocks = width // LANES
    modes = 2 * pairs
    vmem = pl.BlockSpec(memory_space=pltpu.VMEM)
    result = pl.pallas_call(
        functools.partial(row_kernel, seg_count),
        out_shape=jax.ShapeDtypeStruct((3, levels, width), jnp.bfloat16),
        in_specs=[pl.BlockSpec(memory_space=pltpu.SMEM)] + [vmem] * 4,
        out_specs=vmem,
        scratch_shapes=[
            pltpu.VMEM((SPAN, 2 * modes), jnp.bfloat16),
            pltpu.VMEM((16, modes), jnp.float32),
            pltpu.VMEM((16, modes), jnp.float32),
            pltpu.VMEM((blocks * 3 * levels, 2 * modes), jnp.float32),
            pltpu.VMEM((blocks * 3 * levels, 2 * LANES), jnp.float32),
        ],
        compiler_params=pltpu.CompilerParams(vmem_limit_bytes=40 * 1024 * 1024),
    )(
        row_lengths,
        pair_waves[None, :],
        whole,
        departure[0, :, 0, :],
        weights[:, 0, :, 0, :],
    )
    return result[:, None, :, None, :]


def solution(mesh):
    return jax.shard_map(
        local,
        mesh=mesh,
        in_specs=(
            P("wave", None, None, "lon", None),
            P("wave", None, None),
            P(),
            P("wave"),
            P("wave", None, "lon", None),
            P(None, "wave", None, "lon", None),
        ),
        out_specs=P(None, "wave", None, "lon", None),
        check_vma=False,
    )
```

```python
import functools
import math

import jax
import jax.numpy as jnp
import numpy as np
from jax import lax
from jax.experimental import pallas as pl
from jax.experimental.pallas import tpu as pltpu
from jax.sharding import PartitionSpec as P

TRUNC = 1279
HALO = 8
LANES = 128
SHIFTS = 2 * HALO + 1
SPAN = LANES + 2 * HALO


def unit_circle(waves, points, length, inverse):
    product = waves * points
    turns = jnp.floor(product * inverse + 0.5)
    half = (product - turns * length) * (inverse * math.pi)
    sq = half * half
    sine, cosine = 0.0, 0.0
    for k in range(7, -1, -1):
        sine = sine * sq + (-1.0) ** k / math.factorial(2 * k + 1)
        cosine = cosine * sq + (-1.0) ** k / math.factorial(2 * k)
    sine = sine * half
    return 1.0 - 2.0 * sine * sine, 2.0 * sine * cosine


def make_tables(seg_count, pairs_ref, length, table_ref, start_cos, start_sin):
    first = pairs_ref[...].astype(jnp.float32)
    waves = jnp.concatenate([first, TRUNC - first], axis=1)
    modes = waves.shape[1]
    length_f = length.astype(jnp.float32)
    inverse = 1.0 / jnp.full((1, 1), length_f, jnp.float32)
    fine_at = lax.broadcasted_iota(jnp.int32, (16, modes), 0).astype(jnp.float32)
    cos_f, sin_f = unit_circle(waves, fine_at, length_f, inverse)
    cos_c, sin_c = unit_circle(waves, fine_at * 16.0, length_f, inverse)
    for a in range(SPAN // 16):
        ca, sa = cos_c[a : a + 1], sin_c[a : a + 1]
        rows = slice(16 * a, 16 * a + 16)
        table_ref[rows, :modes] = (cos_f * ca - sin_f * sa).astype(jnp.bfloat16)
        table_ref[rows, modes:] = (-(sin_f * ca + cos_f * sa)).astype(jnp.bfloat16)
    share = length // seg_count
    start = (lax.axis_index("lon") * share - HALO).astype(jnp.float32)
    cos_s, sin_s = unit_circle(waves, fine_at * float(LANES) + start, length_f, inverse)
    highest = (length // 2 - 1).astype(jnp.float32)
    factor = jnp.where(waves == 0.0, 1.0, jnp.where(waves <= highest, 2.0, 0.0))
    start_cos[...] = cos_s * factor
    start_sin[...] = sin_s * factor


def synthesize(real, imag, blocks, table_ref, start_cos, start_sin, lhs_ref, grid_ref):
    rows, modes = real.shape
    for h in range(blocks):
        c, s = start_cos[h : h + 1], start_sin[h : h + 1]
        at = slice(h * rows, (h + 1) * rows)
        lhs_ref[at, :modes] = real * c - imag * s
        lhs_ref[at, modes:] = real * s + imag * c
    grid_ref[:, :SPAN] = lax.dot_general(
        lhs_ref[...].astype(jnp.bfloat16),
        table_ref[...],
        (((1,), (1,)), ((), ())),
        preferred_element_type=jnp.float32,
    )


def depart(share, blocks, levels, departure_ref, weights_ref, grid_ref, out_ref):
    rows = 3 * levels
    for h in range(blocks):
        lanes = slice(h * LANES, (h + 1) * LANES)
        cell = departure_ref[:, lanes]
        factors = [weights_ref[c, :, lanes].astype(jnp.float32) for c in range(4)]
        totals = [jnp.zeros((levels, LANES), jnp.float32)] * 3
        for s in range(SHIFTS):
            weight = jnp.zeros((levels, LANES), jnp.float32)
            for c in range(4):
                if 1 - HALO <= s - 7 - c <= HALO - 2:
                    weight = weight + jnp.where(cell == s - 7 - c, factors[c], 0.0)
            moved = grid_ref[h * rows : (h + 1) * rows, s : s + LANES]
            for f in range(3):
                totals[f] = totals[f] + weight * moved[f * levels : (f + 1) * levels]
        slot = h * LANES + lax.broadcasted_iota(jnp.int32, (levels, LANES), 1)
        for f in range(3):
            kept = jnp.where(slot < share, totals[f], 0.0)
            out_ref[f, :, lanes] = kept.astype(jnp.bfloat16)


def exchange(send_ref, recv_ref, send_sem, recv_sem):
    along = lax.axis_size("lon")
    total = lax.axis_size("wave") * along
    me = lax.axis_index("wave") * along + lax.axis_index("lon")

    def target_of(step):
        target = lax.rem(me + step, total)
        return lax.div(target, along), lax.rem(target, along)

    def copy_at(step):
        row, place = target_of(step)
        return pltpu.make_async_remote_copy(
            src_ref=send_ref.at[row],
            dst_ref=recv_ref.at[me],
            send_sem=send_sem.at[step],
            recv_sem=recv_sem.at[step],
            device_id=(row, place),
            device_id_type=pl.DeviceIdType.MESH,
        )

    def greet():
        barrier = pltpu.get_barrier_semaphore()

        def one(step, carry):
            pl.semaphore_signal(
                barrier, inc=1, device_id=target_of(step), device_id_type=pl.DeviceIdType.MESH
            )
            return carry

        lax.fori_loop(1, total, one, 0)

    def start():
        pl.semaphore_wait(pltpu.get_barrier_semaphore(), total - 1)

        def one(step, carry):
            copy_at(step).start()
            return carry

        lax.fori_loop(1, total, one, 0)
        recv_ref[me] = send_ref[lax.axis_index("wave")]

    def finish():
        def one(step, carry):
            copy_at(step).wait()
            return carry

        lax.fori_loop(1, total, one, 0)

    return greet, start, finish


def row_kernel(
    seg_count, length_ref, pairs_ref, send_ref, order_ref, departure_ref, weights_ref, out_ref,
    table_ref, start_cos, start_sin, lhs_ref, grid_ref, recv_ref, fourier_ref, send_sem, recv_sem,
):
    length = length_ref[0]
    levels, width = departure_ref.shape
    blocks = width // LANES
    greet, start, finish = exchange(send_ref, recv_ref, send_sem, recv_sem)
    greet()
    start()
    make_tables(seg_count, pairs_ref, length, table_ref, start_cos, start_sin)
    finish()
    along = lax.axis_size("lon")
    waves = lax.axis_size("wave")
    pair_dev = pairs_ref.shape[1] // waves
    for i in range(waves):
        parts = jnp.concatenate([recv_ref[i * along + g] for g in range(along)], axis=0)
        ordered = jnp.dot(order_ref[...], parts, preferred_element_type=jnp.float32)
        for s in range(2):
            at = (s * waves + i) * pair_dev
            fourier_ref[:, at : at + pair_dev] = ordered[:, s * pair_dev : (s + 1) * pair_dev]
    real = fourier_ref[: 3 * levels]
    imag = fourier_ref[3 * levels :]
    synthesize(real, imag, blocks, table_ref, start_cos, start_sin, lhs_ref, grid_ref)
    depart(length // seg_count, blocks, levels, departure_ref, weights_ref, grid_ref, out_ref)


def row_order(levels, level_dev, chunk):
    order = np.zeros((6 * levels, levels // level_dev * chunk), np.float32)
    for part_field in range(6):
        for v in range(levels):
            source = v // level_dev * chunk + part_field * level_dev + v % level_dev
            order[part_field * levels + v, source] = 1.0
    return jnp.asarray(order, jnp.bfloat16)


def local(spectra, legendre, pair_waves, row_lengths, departure, weights):
    pair_dev = spectra.shape[0]
    level_dev = spectra.shape[3]
    packed = spectra.shape[4]
    row_total = legendre.shape[1]
    pairs = pair_waves.shape[0]
    levels, width = departure.shape[1], departure.shape[3]
    seg_count = lax.axis_size("lon")
    columns = 6 * level_dev
    start_pair = lax.axis_index("wave") * pair_dev
    own_waves = lax.dynamic_slice_in_dim(pair_waves, start_pair, pair_dev)
    flat_spec = spectra.reshape(pair_dev, columns, packed)
    keeper = jnp.arange(packed, dtype=jnp.int32)[None, :] < (TRUNC + 1 - own_waves)[:, None]
    keeper = keeper[:, None, :]
    blank = jnp.zeros_like(flat_spec)
    doubled = jnp.stack(
        [jnp.where(keeper, flat_spec, blank), jnp.where(keeper, blank, flat_spec)], axis=1
    )
    fourier = jnp.einsum("pwcn,pln->pwcl", doubled, legendre, preferred_element_type=jnp.float32)
    chunk = -(-columns // 16) * 16
    send = jnp.transpose(fourier.astype(jnp.bfloat16), (3, 2, 1, 0))
    send = send.reshape(row_total, columns, 2 * pair_dev)
    send = jnp.pad(send, ((0, 0), (0, chunk - columns), (0, 0)))
    devices = lax.axis_size("wave") * seg_count
    blocks = width // LANES
    modes = 2 * pairs
    vmem = pl.BlockSpec(memory_space=pltpu.VMEM)
    result = pl.pallas_call(
        functools.partial(row_kernel, seg_count),
        out_shape=jax.ShapeDtypeStruct((3, levels, width), jnp.bfloat16),
        in_specs=[pl.BlockSpec(memory_space=pltpu.SMEM)] + [vmem] * 5,
        out_specs=vmem,
        scratch_shapes=[
            pltpu.VMEM((SPAN, 2 * modes), jnp.bfloat16),
            pltpu.VMEM((16, modes), jnp.float32),
            pltpu.VMEM((16, modes), jnp.float32),
            pltpu.VMEM((blocks * 3 * levels, 2 * modes), jnp.float32),
            pltpu.VMEM((blocks * 3 * levels, 2 * LANES), jnp.float32),
            pltpu.VMEM((devices, chunk, 2 * pair_dev), jnp.bfloat16),
            pltpu.VMEM((6 * levels, modes), jnp.float32),
            pltpu.SemaphoreType.DMA((devices,)),
            pltpu.SemaphoreType.DMA((devices,)),
        ],
        compiler_params=pltpu.CompilerParams(
            vmem_limit_bytes=40 * 1024 * 1024, collective_id=0, has_side_effects=True
        ),
    )(
        row_lengths,
        pair_waves[None, :],
        send,
        row_order(levels, level_dev, chunk),
        departure[0, :, 0, :],
        weights[:, 0, :, 0, :],
    )
    return result[:, None, :, None, :]


def solution(mesh):
    return jax.shard_map(
        local,
        mesh=mesh,
        in_specs=(
            P("wave", None, None, "lon", None),
            P("wave", None, None),
            P(),
            P("wave"),
            P("wave", None, "lon", None),
            P(None, "wave", None, "lon", None),
        ),
        out_specs=P(None, "wave", None, "lon", None),
        check_vma=False,
    )
```

```python
import functools
import math

import jax
import jax.numpy as jnp
import numpy as np
from jax import lax
from jax.experimental import pallas as pl
from jax.experimental.pallas import tpu as pltpu
from jax.sharding import PartitionSpec as P

TRUNC = 1279
HALO = 8
LANES = 128
GROUP = 16
SHIFTS = 2 * HALO + 1
SPAN = LANES + 2 * HALO


def unit_circle(waves, points, length, inverse):
    product = waves * points
    turns = jnp.floor(product * inverse + 0.5)
    half = (product - turns * length) * (inverse * math.pi)
    sq = half * half
    sine, cosine = 0.0, 0.0
    for k in range(7, -1, -1):
        sine = sine * sq + (-1.0) ** k / math.factorial(2 * k + 1)
        cosine = cosine * sq + (-1.0) ** k / math.factorial(2 * k)
    sine = sine * half
    return 1.0 - 2.0 * sine * sine, 2.0 * sine * cosine


def make_tables(seg_count, pairs_ref, length, table_ref, start_cos, start_sin):
    first = pairs_ref[...].astype(jnp.float32)
    waves = jnp.concatenate([first, TRUNC - first], axis=1)
    modes = waves.shape[1]
    length_f = length.astype(jnp.float32)
    inverse = 1.0 / jnp.full((1, 1), length_f, jnp.float32)
    fine_at = lax.broadcasted_iota(jnp.int32, (16, modes), 0).astype(jnp.float32)
    cos_f, sin_f = unit_circle(waves, fine_at, length_f, inverse)
    cos_c, sin_c = unit_circle(waves, fine_at * 16.0, length_f, inverse)
    for a in range(SPAN // 16):
        ca, sa = cos_c[a : a + 1], sin_c[a : a + 1]
        rows = slice(16 * a, 16 * a + 16)
        table_ref[rows, :modes] = (cos_f * ca - sin_f * sa).astype(jnp.bfloat16)
        table_ref[rows, modes:] = (-(sin_f * ca + cos_f * sa)).astype(jnp.bfloat16)
    share = length // seg_count
    start = (lax.axis_index("lon") * share - HALO).astype(jnp.float32)
    cos_s, sin_s = unit_circle(waves, fine_at * float(LANES) + start, length_f, inverse)
    highest = (length // 2 - 1).astype(jnp.float32)
    factor = jnp.where(waves == 0.0, 1.0, jnp.where(waves <= highest, 2.0, 0.0))
    start_cos[...] = cos_s * factor
    start_sin[...] = sin_s * factor


def synthesize(real, imag, blocks, table_ref, start_cos, start_sin, lhs_ref, grid_ref):
    rows, modes = real.shape
    for h in range(blocks):
        c, s = start_cos[h : h + 1], start_sin[h : h + 1]
        at = slice(h * rows, (h + 1) * rows)
        lhs_ref[at, :modes] = real * c - imag * s
        lhs_ref[at, modes:] = real * s + imag * c
    grid_ref[:, :SPAN] = lax.dot_general(
        lhs_ref[...].astype(jnp.bfloat16),
        table_ref[...],
        (((1,), (1,)), ((), ())),
        preferred_element_type=jnp.float32,
    )


def depart(share, blocks, levels, departure_ref, weights_ref, grid_ref, out_ref):
    rows = 3 * levels
    for h in range(blocks):
        lanes = slice(h * LANES, (h + 1) * LANES)
        cell = departure_ref[:, lanes]
        factors = [weights_ref[c, :, lanes].astype(jnp.float32) for c in range(4)]
        totals = [jnp.zeros((levels, LANES), jnp.float32)] * 3
        for s in range(SHIFTS):
            weight = jnp.zeros((levels, LANES), jnp.float32)
            for c in range(4):
                if 1 - HALO <= s - 7 - c <= HALO - 2:
                    weight = weight + jnp.where(cell == s - 7 - c, factors[c], 0.0)
            moved = grid_ref[h * rows : (h + 1) * rows, s : s + LANES]
            for f in range(3):
                totals[f] = totals[f] + weight * moved[f * levels : (f + 1) * levels]
        slot = h * LANES + lax.broadcasted_iota(jnp.int32, (levels, LANES), 1)
        for f in range(3):
            kept = jnp.where(slot < share, totals[f], 0.0)
            out_ref[f, :, lanes] = kept.astype(jnp.bfloat16)


def exchange(send_ref, recv_ref, send_sem, recv_sem):
    along = lax.axis_size("lon")
    total = lax.axis_size("wave") * along
    me = lax.axis_index("wave") * along + lax.axis_index("lon")

    def target_of(step):
        target = lax.rem(me + step, total)
        return lax.div(target, along), lax.rem(target, along)

    def copy_at(step):
        row, place = target_of(step)
        return pltpu.make_async_remote_copy(
            src_ref=send_ref.at[row],
            dst_ref=recv_ref.at[me],
            send_sem=send_sem.at[step],
            recv_sem=recv_sem.at[step],
            device_id=(row, place),
            device_id_type=pl.DeviceIdType.MESH,
        )

    def greet():
        barrier = pltpu.get_barrier_semaphore()

        def one(step, carry):
            pl.semaphore_signal(
                barrier, inc=1, device_id=target_of(step), device_id_type=pl.DeviceIdType.MESH
            )
            return carry

        lax.fori_loop(1, total, one, 0)

    def start():
        pl.semaphore_wait(pltpu.get_barrier_semaphore(), total - 1)

        def one(step, carry):
            copy_at(step).start()
            return carry

        lax.fori_loop(1, total, one, 0)
        recv_ref[me] = send_ref[lax.axis_index("wave")]

    def finish():
        def one(step, carry):
            copy_at(step).wait()
            return carry

        lax.fori_loop(1, total, one, 0)

    return greet, start, finish


def row_kernel(
    seg_count, length_ref, pairs_ref, send_ref, order_ref, departure_ref, weights_ref, out_ref,
    table_ref, start_cos, start_sin, lhs_ref, grid_ref, recv_ref, fourier_ref, send_sem, recv_sem,
):
    length = length_ref[0]
    levels, width = departure_ref.shape
    blocks = width // LANES
    greet, start, finish = exchange(send_ref, recv_ref, send_sem, recv_sem)
    greet()
    start()
    make_tables(seg_count, pairs_ref, length, table_ref, start_cos, start_sin)
    finish()
    along = lax.axis_size("lon")
    waves = lax.axis_size("wave")
    pair_dev = pairs_ref.shape[1] // waves
    for i in range(waves):
        parts = jnp.concatenate([recv_ref[i * along + g] for g in range(along)], axis=0)
        ordered = jnp.dot(order_ref[...], parts, preferred_element_type=jnp.float32)
        for s in range(2):
            at = (s * waves + i) * pair_dev
            fourier_ref[:, at : at + pair_dev] = ordered[:, s * pair_dev : (s + 1) * pair_dev]
    real = fourier_ref[: 3 * levels]
    imag = fourier_ref[3 * levels :]
    synthesize(real, imag, blocks, table_ref, start_cos, start_sin, lhs_ref, grid_ref)
    depart(length // seg_count, blocks, levels, departure_ref, weights_ref, grid_ref, out_ref)


def legendre_kernel(
    pair_dev, pairs_ref, spectra_ref, legendre_ref, spread_ref, send_ref, rhs_ref, send_f
):
    columns, padded, packed = spectra_ref.shape
    row_total = legendre_ref.shape[1]
    chunk = send_ref.shape[1]
    start = lax.axis_index("wave") * pair_dev
    lane = lax.broadcasted_iota(jnp.int32, (row_total, packed), 1)
    zero = jnp.zeros((row_total, packed), jnp.float32)
    wide = 2 * GROUP * row_total
    own = lax.broadcasted_iota(jnp.int32, (GROUP, wide), 0)
    other = lax.broadcasted_iota(jnp.int32, (GROUP, wide), 1)
    low = jnp.where(other >= wide // 2, other - wide // 2, other) - own * row_total
    mine = jnp.where((low >= 0) & (low < row_total), 1.0, 0.0)[None]
    send_f[...] = jnp.zeros_like(send_f)
    for g in range(padded // GROUP):
        for p in range(0, GROUP, 2):
            first, second = [], []
            for at in (g * GROUP + p, g * GROUP + p + 1):
                if at < pair_dev:
                    rows = legendre_ref[at].astype(jnp.float32)
                    keep = lane < TRUNC + 1 - pairs_ref[start + at]
                    first.append(jnp.where(keep, rows, 0.0))
                    second.append(jnp.where(keep, 0.0, rows))
                else:
                    first.append(zero)
                    second.append(zero)
            for s, part in enumerate((first, second)):
                at = (s * GROUP + p) * row_total
                part = jnp.concatenate(part, axis=0).astype(jnp.bfloat16)
                rhs_ref[g, at : at + 2 * row_total] = part
        lhs = spectra_ref[:, g * GROUP : (g + 1) * GROUP, :].reshape(columns * GROUP, packed)
        cross = lax.dot_general(
            lhs, rhs_ref[g], (((1,), (1,)), ((), ())), preferred_element_type=jnp.float32
        )
        sums = jnp.sum(cross.reshape(columns, GROUP, wide) * mine, axis=1).astype(jnp.bfloat16)
        by_row = jnp.dot(sums, spread_ref[...], preferred_element_type=jnp.float32)
        valid = min(GROUP, pair_dev - g * GROUP)
        for j in range(row_total):
            for s in range(2):
                source = (j * 2 + s) * GROUP
                to = s * pair_dev + g * GROUP
                send_f[j, :columns, to : to + valid] = by_row[:, source : source + valid]
    for j in range(row_total):
        send_ref[j] = send_f[j].astype(jnp.bfloat16)


def lane_order(row_total):
    wide = 2 * GROUP * row_total
    source = np.arange(wide).reshape(2, GROUP, row_total).transpose(2, 0, 1).reshape(-1)
    order = np.zeros((wide, wide), np.float32)
    order[source, np.arange(wide)] = 1.0
    return jnp.asarray(order, jnp.bfloat16)


def row_order(levels, level_dev, chunk):
    order = np.zeros((6 * levels, levels // level_dev * chunk), np.float32)
    for part_field in range(6):
        for v in range(levels):
            source = v // level_dev * chunk + part_field * level_dev + v % level_dev
            order[part_field * levels + v, source] = 1.0
    return jnp.asarray(order, jnp.bfloat16)


def local(spectra, legendre, pair_waves, row_lengths, departure, weights):
    pair_dev = spectra.shape[0]
    level_dev = spectra.shape[3]
    packed = spectra.shape[4]
    row_total = legendre.shape[1]
    pairs = pair_waves.shape[0]
    levels, width = departure.shape[1], departure.shape[3]
    seg_count = lax.axis_size("lon")
    columns = 6 * level_dev
    padded = -(-pair_dev // GROUP) * GROUP
    chunk = -(-columns // 16) * 16
    flat_spec = jnp.transpose(spectra, (1, 2, 3, 0, 4)).reshape(columns, pair_dev, packed)
    flat_spec = jnp.pad(flat_spec, ((0, 0), (0, padded - pair_dev), (0, 0)))
    vmem = pl.BlockSpec(memory_space=pltpu.VMEM)
    smem = pl.BlockSpec(memory_space=pltpu.SMEM)
    wide = 2 * GROUP * row_total
    send = pl.pallas_call(
        functools.partial(legendre_kernel, pair_dev),
        out_shape=jax.ShapeDtypeStruct((row_total, chunk, 2 * pair_dev), jnp.bfloat16),
        in_specs=[smem] + [vmem] * 3,
        out_specs=vmem,
        scratch_shapes=[
            pltpu.VMEM((padded // GROUP, wide, packed), jnp.bfloat16),
            pltpu.VMEM((row_total, chunk, 2 * pair_dev), jnp.float32),
        ],
        compiler_params=pltpu.CompilerParams(vmem_limit_bytes=40 * 1024 * 1024),
    )(pair_waves, flat_spec, legendre, lane_order(row_total))
    devices = lax.axis_size("wave") * seg_count
    blocks = width // LANES
    modes = 2 * pairs
    result = pl.pallas_call(
        functools.partial(row_kernel, seg_count),
        out_shape=jax.ShapeDtypeStruct((3, levels, width), jnp.bfloat16),
        in_specs=[smem] + [vmem] * 5,
        out_specs=vmem,
        scratch_shapes=[
            pltpu.VMEM((SPAN, 2 * modes), jnp.bfloat16),
            pltpu.VMEM((16, modes), jnp.float32),
            pltpu.VMEM((16, modes), jnp.float32),
            pltpu.VMEM((blocks * 3 * levels, 2 * modes), jnp.float32),
            pltpu.VMEM((blocks * 3 * levels, 2 * LANES), jnp.float32),
            pltpu.VMEM((devices, chunk, 2 * pair_dev), jnp.bfloat16),
            pltpu.VMEM((6 * levels, modes), jnp.float32),
            pltpu.SemaphoreType.DMA((devices,)),
            pltpu.SemaphoreType.DMA((devices,)),
        ],
        compiler_params=pltpu.CompilerParams(
            vmem_limit_bytes=40 * 1024 * 1024, collective_id=0, has_side_effects=True
        ),
    )(
        row_lengths,
        pair_waves[None, :],
        send,
        row_order(levels, level_dev, chunk),
        departure[0, :, 0, :],
        weights[:, 0, :, 0, :],
    )
    return result[:, None, :, None, :]


def solution(mesh):
    return jax.shard_map(
        local,
        mesh=mesh,
        in_specs=(
            P("wave", None, None, "lon", None),
            P("wave", None, None),
            P(),
            P("wave"),
            P("wave", None, "lon", None),
            P(None, "wave", None, "lon", None),
        ),
        out_specs=P(None, "wave", None, "lon", None),
        check_vma=False,
    )
```

```python
import functools
import math

import jax
import jax.numpy as jnp
import numpy as np
from jax import lax
from jax.experimental import pallas as pl
from jax.experimental.pallas import tpu as pltpu
from jax.sharding import PartitionSpec as P

TRUNC = 1279
HALO = 8
LANES = 128
GROUP = 16
SHIFTS = 2 * HALO + 1
SPAN = LANES + 2 * HALO


def unit_circle(waves, points, length, inverse):
    product = waves * points
    turns = jnp.floor(product * inverse + 0.5)
    half = (product - turns * length) * (inverse * math.pi)
    sq = half * half
    sine, cosine = 0.0, 0.0
    for k in range(7, -1, -1):
        sine = sine * sq + (-1.0) ** k / math.factorial(2 * k + 1)
        cosine = cosine * sq + (-1.0) ** k / math.factorial(2 * k)
    sine = sine * half
    return 1.0 - 2.0 * sine * sine, 2.0 * sine * cosine


def make_tables(seg_count, pairs_ref, length, table_ref, start_cos, start_sin):
    first = pairs_ref[...].astype(jnp.float32)
    waves = jnp.concatenate([first, TRUNC - first], axis=1)
    modes = waves.shape[1]
    length_f = length.astype(jnp.float32)
    inverse = 1.0 / jnp.full((1, 1), length_f, jnp.float32)
    fine_at = lax.broadcasted_iota(jnp.int32, (16, modes), 0).astype(jnp.float32)
    cos_f, sin_f = unit_circle(waves, fine_at, length_f, inverse)
    cos_c, sin_c = unit_circle(waves, fine_at * 16.0, length_f, inverse)
    for a in range(SPAN // 16):
        ca, sa = cos_c[a : a + 1], sin_c[a : a + 1]
        rows = slice(16 * a, 16 * a + 16)
        table_ref[rows, :modes] = (cos_f * ca - sin_f * sa).astype(jnp.bfloat16)
        table_ref[rows, modes:] = (-(sin_f * ca + cos_f * sa)).astype(jnp.bfloat16)
    share = length // seg_count
    start = (lax.axis_index("lon") * share - HALO).astype(jnp.float32)
    cos_s, sin_s = unit_circle(waves, fine_at * float(LANES) + start, length_f, inverse)
    highest = (length // 2 - 1).astype(jnp.float32)
    factor = jnp.where(waves == 0.0, 1.0, jnp.where(waves <= highest, 2.0, 0.0))
    start_cos[...] = cos_s * factor
    start_sin[...] = sin_s * factor


def synthesize(real, imag, blocks, table_ref, start_cos, start_sin, lhs_ref, grid_ref):
    rows, modes = real.shape
    for h in range(blocks):
        c, s = start_cos[h : h + 1], start_sin[h : h + 1]
        at = slice(h * rows, (h + 1) * rows)
        lhs_ref[at, :modes] = real * c - imag * s
        lhs_ref[at, modes:] = real * s + imag * c
    grid_ref[:, :SPAN] = lax.dot_general(
        lhs_ref[...].astype(jnp.bfloat16),
        table_ref[...],
        (((1,), (1,)), ((), ())),
        preferred_element_type=jnp.float32,
    )


def depart(share, blocks, levels, departure_ref, weights_ref, grid_ref, out_ref):
    rows = 3 * levels
    for h in range(blocks):
        lanes = slice(h * LANES, (h + 1) * LANES)
        cell = departure_ref[:, lanes]
        factors = [weights_ref[c, :, lanes].astype(jnp.float32) for c in range(4)]
        totals = [jnp.zeros((levels, LANES), jnp.float32)] * 3
        for s in range(SHIFTS):
            weight = jnp.zeros((levels, LANES), jnp.float32)
            for c in range(4):
                if 1 - HALO <= s - 7 - c <= HALO - 2:
                    weight = weight + jnp.where(cell == s - 7 - c, factors[c], 0.0)
            moved = grid_ref[h * rows : (h + 1) * rows, s : s + LANES]
            for f in range(3):
                totals[f] = totals[f] + weight * moved[f * levels : (f + 1) * levels]
        slot = h * LANES + lax.broadcasted_iota(jnp.int32, (levels, LANES), 1)
        for f in range(3):
            kept = jnp.where(slot < share, totals[f], 0.0)
            out_ref[f, :, lanes] = kept.astype(jnp.bfloat16)


def exchange(send_ref, recv_ref, send_sems, recv_sems):
    rows = lax.axis_size("wave")
    chips = lax.axis_size("lon") // 2
    row, place = lax.axis_index("wave"), lax.axis_index("lon")
    chip, core = lax.div(place, 2), lax.rem(place, 2)

    def remote(phase, slot, source, to, device):
        return pltpu.make_async_remote_copy(
            src_ref=source,
            dst_ref=to,
            send_sem=send_sems[phase].at[slot],
            recv_sem=recv_sems[phase].at[slot],
            device_id=device,
            device_id_type=pl.DeviceIdType.MESH,
        )

    def along_wave(step):
        target = lax.rem(row + step, rows)
        return remote(
            0, step, send_ref.at[target], recv_ref.at[place, row], (target, place)
        )

    def chip_at(step):
        return (row, lax.rem(chip + step, chips) * 2 + core)

    def along_chips(step, away):
        maker = lax.rem(row + rows - step, rows)
        block = recv_ref.at[place, maker]
        return remote(1, away * rows + step, block, block, chip_at(away))

    def to_sibling(away):
        block = recv_ref.at[lax.rem(chip + chips - away, chips) * 2 + core]
        return remote(2, away, block, block, (row, chip * 2 + 1 - core))

    def loop(first, last, body):
        def one(step, carry):
            body(step)
            return carry

        lax.fori_loop(first, last, one, 0)

    def greet():
        barrier = pltpu.get_barrier_semaphore()

        def signal(device):
            pl.semaphore_signal(
                barrier, inc=1, device_id=device, device_id_type=pl.DeviceIdType.MESH
            )

        loop(1, rows, lambda step: signal((lax.rem(row + step, rows), place)))
        for away in range(1, chips):
            signal(chip_at(away))
        signal((row, chip * 2 + 1 - core))

    def start():
        pl.semaphore_wait(pltpu.get_barrier_semaphore(), rows + chips - 1)
        loop(1, rows, lambda step: along_wave(step).start())
        recv_ref[place, row] = send_ref[row]
        for away in range(1, chips):
            along_chips(0, away).start()

    def finish():
        def pass_on(step):
            along_wave(step).wait_recv()
            for away in range(1, chips):
                along_chips(step, away).start()

        loop(1, rows, pass_on)
        to_sibling(0).start()
        for away in range(1, chips):
            loop(0, rows, lambda step: along_chips(step, away).wait_recv())
            to_sibling(away).start()
        for away in range(chips):
            to_sibling(away).wait()
        loop(1, rows, lambda step: along_wave(step).wait_send())
        for away in range(1, chips):
            loop(0, rows, lambda step: along_chips(step, away).wait_send())

    return greet, start, finish


def row_kernel(
    seg_count, length_ref, pairs_ref, send_ref, order_ref, departure_ref, weights_ref, out_ref,
    table_ref, start_cos, start_sin, lhs_ref, grid_ref, recv_ref, fourier_ref, *sems,
):
    length = length_ref[0]
    levels, width = departure_ref.shape
    blocks = width // LANES
    greet, start, finish = exchange(send_ref, recv_ref, sems[:3], sems[3:])
    greet()
    start()
    make_tables(seg_count, pairs_ref, length, table_ref, start_cos, start_sin)
    finish()
    along = lax.axis_size("lon")
    waves = lax.axis_size("wave")
    pair_dev = pairs_ref.shape[1] // waves
    for i in range(waves):
        parts = jnp.concatenate([recv_ref[g, i] for g in range(along)], axis=0)
        ordered = jnp.dot(order_ref[...], parts, preferred_element_type=jnp.float32)
        for s in range(2):
            at = (s * waves + i) * pair_dev
            fourier_ref[:, at : at + pair_dev] = ordered[:, s * pair_dev : (s + 1) * pair_dev]
    real = fourier_ref[: 3 * levels]
    imag = fourier_ref[3 * levels :]
    synthesize(real, imag, blocks, table_ref, start_cos, start_sin, lhs_ref, grid_ref)
    depart(length // seg_count, blocks, levels, departure_ref, weights_ref, grid_ref, out_ref)


def legendre_kernel(
    pair_dev, pairs_ref, spectra_ref, legendre_ref, spread_ref, send_ref, rhs_ref, send_f
):
    columns, padded, packed = spectra_ref.shape
    row_total = legendre_ref.shape[1]
    chunk = send_ref.shape[1]
    start = lax.axis_index("wave") * pair_dev
    lane = lax.broadcasted_iota(jnp.int32, (row_total, packed), 1)
    zero = jnp.zeros((row_total, packed), jnp.float32)
    wide = 2 * GROUP * row_total
    own = lax.broadcasted_iota(jnp.int32, (GROUP, wide), 0)
    other = lax.broadcasted_iota(jnp.int32, (GROUP, wide), 1)
    low = jnp.where(other >= wide // 2, other - wide // 2, other) - own * row_total
    mine = jnp.where((low >= 0) & (low < row_total), 1.0, 0.0)[None]
    send_f[...] = jnp.zeros_like(send_f)
    for g in range(padded // GROUP):
        for p in range(0, GROUP, 2):
            first, second = [], []
            for at in (g * GROUP + p, g * GROUP + p + 1):
                if at < pair_dev:
                    rows = legendre_ref[at].astype(jnp.float32)
                    keep = lane < TRUNC + 1 - pairs_ref[start + at]
                    first.append(jnp.where(keep, rows, 0.0))
                    second.append(jnp.where(keep, 0.0, rows))
                else:
                    first.append(zero)
                    second.append(zero)
            for s, part in enumerate((first, second)):
                at = (s * GROUP + p) * row_total
                part = jnp.concatenate(part, axis=0).astype(jnp.bfloat16)
                rhs_ref[g, at : at + 2 * row_total] = part
        lhs = spectra_ref[:, g * GROUP : (g + 1) * GROUP, :].reshape(columns * GROUP, packed)
        cross = lax.dot_general(
            lhs, rhs_ref[g], (((1,), (1,)), ((), ())), preferred_element_type=jnp.float32
        )
        sums = jnp.sum(cross.reshape(columns, GROUP, wide) * mine, axis=1).astype(jnp.bfloat16)
        by_row = jnp.dot(sums, spread_ref[...], preferred_element_type=jnp.float32)
        valid = min(GROUP, pair_dev - g * GROUP)
        for j in range(row_total):
            for s in range(2):
                source = (j * 2 + s) * GROUP
                to = s * pair_dev + g * GROUP
                send_f[j, :columns, to : to + valid] = by_row[:, source : source + valid]
    for j in range(row_total):
        send_ref[j] = send_f[j].astype(jnp.bfloat16)


def lane_order(row_total):
    wide = 2 * GROUP * row_total
    source = np.arange(wide).reshape(2, GROUP, row_total).transpose(2, 0, 1).reshape(-1)
    order = np.zeros((wide, wide), np.float32)
    order[source, np.arange(wide)] = 1.0
    return jnp.asarray(order, jnp.bfloat16)


def row_order(levels, level_dev, chunk):
    order = np.zeros((6 * levels, levels // level_dev * chunk), np.float32)
    for part_field in range(6):
        for v in range(levels):
            source = v // level_dev * chunk + part_field * level_dev + v % level_dev
            order[part_field * levels + v, source] = 1.0
    return jnp.asarray(order, jnp.bfloat16)


def local(spectra, legendre, pair_waves, row_lengths, departure, weights):
    pair_dev = spectra.shape[0]
    level_dev = spectra.shape[3]
    packed = spectra.shape[4]
    row_total = legendre.shape[1]
    pairs = pair_waves.shape[0]
    levels, width = departure.shape[1], departure.shape[3]
    seg_count = lax.axis_size("lon")
    columns = 6 * level_dev
    padded = -(-pair_dev // GROUP) * GROUP
    chunk = -(-columns // 16) * 16
    flat_spec = jnp.transpose(spectra, (1, 2, 3, 0, 4)).reshape(columns, pair_dev, packed)
    flat_spec = jnp.pad(flat_spec, ((0, 0), (0, padded - pair_dev), (0, 0)))
    vmem = pl.BlockSpec(memory_space=pltpu.VMEM)
    smem = pl.BlockSpec(memory_space=pltpu.SMEM)
    wide = 2 * GROUP * row_total
    send = pl.pallas_call(
        functools.partial(legendre_kernel, pair_dev),
        out_shape=jax.ShapeDtypeStruct((row_total, chunk, 2 * pair_dev), jnp.bfloat16),
        in_specs=[smem] + [vmem] * 3,
        out_specs=vmem,
        scratch_shapes=[
            pltpu.VMEM((padded // GROUP, wide, packed), jnp.bfloat16),
            pltpu.VMEM((row_total, chunk, 2 * pair_dev), jnp.float32),
        ],
        compiler_params=pltpu.CompilerParams(vmem_limit_bytes=40 * 1024 * 1024),
    )(pair_waves, flat_spec, legendre, lane_order(row_total))
    rows = lax.axis_size("wave")
    counts = (rows, seg_count // 2 * rows, seg_count // 2)
    blocks = width // LANES
    modes = 2 * pairs
    result = pl.pallas_call(
        functools.partial(row_kernel, seg_count),
        out_shape=jax.ShapeDtypeStruct((3, levels, width), jnp.bfloat16),
        in_specs=[smem] + [vmem] * 5,
        out_specs=vmem,
        scratch_shapes=[
            pltpu.VMEM((SPAN, 2 * modes), jnp.bfloat16),
            pltpu.VMEM((16, modes), jnp.float32),
            pltpu.VMEM((16, modes), jnp.float32),
            pltpu.VMEM((blocks * 3 * levels, 2 * modes), jnp.float32),
            pltpu.VMEM((blocks * 3 * levels, 2 * LANES), jnp.float32),
            pltpu.VMEM((seg_count, rows, chunk, 2 * pair_dev), jnp.bfloat16),
            pltpu.VMEM((6 * levels, modes), jnp.float32),
        ]
        + [pltpu.SemaphoreType.DMA((count,)) for count in counts * 2],
        compiler_params=pltpu.CompilerParams(
            vmem_limit_bytes=40 * 1024 * 1024, collective_id=0, has_side_effects=True
        ),
    )(
        row_lengths,
        pair_waves[None, :],
        send,
        row_order(levels, level_dev, chunk),
        departure[0, :, 0, :],
        weights[:, 0, :, 0, :],
    )
    return result[:, None, :, None, :]


def solution(mesh):
    return jax.shard_map(
        local,
        mesh=mesh,
        in_specs=(
            P("wave", None, None, "lon", None),
            P("wave", None, None),
            P(),
            P("wave"),
            P("wave", None, "lon", None),
            P(None, "wave", None, "lon", None),
        ),
        out_specs=P(None, "wave", None, "lon", None),
        check_vma=False,
    )
```

```python
import functools
import math

import jax
import jax.numpy as jnp
import numpy as np
from jax import lax
from jax.experimental import pallas as pl
from jax.experimental.pallas import tpu as pltpu
from jax.sharding import PartitionSpec as P

TRUNC = 1279
HALO = 8
LANES = 128
GROUP = 16
SHIFTS = 2 * HALO + 1
SPAN = LANES + 2 * HALO


def unit_circle(waves, points, length, inverse):
    product = waves * points
    turns = jnp.floor(product * inverse + 0.5)
    half = (product - turns * length) * (inverse * math.pi)
    sq = half * half
    sine, cosine = 0.0, 0.0
    for k in range(7, -1, -1):
        sine = sine * sq + (-1.0) ** k / math.factorial(2 * k + 1)
        cosine = cosine * sq + (-1.0) ** k / math.factorial(2 * k)
    sine = sine * half
    return 1.0 - 2.0 * sine * sine, 2.0 * sine * cosine


def make_tables(seg_count, pairs_ref, length, table_ref, start_cos, start_sin):
    first = pairs_ref[...].astype(jnp.float32)
    waves = jnp.concatenate([first, TRUNC - first], axis=1)
    modes = waves.shape[1]
    length_f = length.astype(jnp.float32)
    inverse = 1.0 / jnp.full((1, 1), length_f, jnp.float32)
    fine_at = lax.broadcasted_iota(jnp.int32, (16, modes), 0).astype(jnp.float32)
    cos_f, sin_f = unit_circle(waves, fine_at, length_f, inverse)
    cos_c, sin_c = unit_circle(waves, fine_at * 16.0, length_f, inverse)
    for a in range(SPAN // 16):
        ca, sa = cos_c[a : a + 1], sin_c[a : a + 1]
        rows = slice(16 * a, 16 * a + 16)
        table_ref[rows, :modes] = (cos_f * ca - sin_f * sa).astype(jnp.bfloat16)
        table_ref[rows, modes:] = (-(sin_f * ca + cos_f * sa)).astype(jnp.bfloat16)
    share = length // seg_count
    start = (lax.axis_index("lon") * share - HALO).astype(jnp.float32)
    cos_s, sin_s = unit_circle(waves, fine_at * float(LANES) + start, length_f, inverse)
    highest = (length // 2 - 1).astype(jnp.float32)
    factor = jnp.where(waves == 0.0, 1.0, jnp.where(waves <= highest, 2.0, 0.0))
    start_cos[...] = cos_s * factor
    start_sin[...] = sin_s * factor


def synthesize(real, imag, blocks, table_ref, start_cos, start_sin, lhs_ref, grid_ref):
    rows, modes = real.shape
    for h in range(blocks):
        c, s = start_cos[h : h + 1], start_sin[h : h + 1]
        at = slice(h * rows, (h + 1) * rows)
        lhs_ref[at, :modes] = real * c - imag * s
        lhs_ref[at, modes:] = real * s + imag * c
    grid_ref[:, :SPAN] = lax.dot_general(
        lhs_ref[...].astype(jnp.bfloat16),
        table_ref[...],
        (((1,), (1,)), ((), ())),
        preferred_element_type=jnp.float32,
    )


def depart(share, blocks, levels, departure_ref, weights_ref, grid_ref, out_ref):
    rows = 3 * levels
    for h in range(blocks):
        lanes = slice(h * LANES, (h + 1) * LANES)
        cell = departure_ref[:, lanes]
        factors = [weights_ref[c, :, lanes].astype(jnp.float32) for c in range(4)]
        totals = [jnp.zeros((levels, LANES), jnp.float32)] * 3
        for s in range(SHIFTS):
            weight = jnp.zeros((levels, LANES), jnp.float32)
            for c in range(4):
                if 1 - HALO <= s - 7 - c <= HALO - 2:
                    weight = weight + jnp.where(cell == s - 7 - c, factors[c], 0.0)
            moved = grid_ref[h * rows : (h + 1) * rows, s : s + LANES]
            for f in range(3):
                totals[f] = totals[f] + weight * moved[f * levels : (f + 1) * levels]
        slot = h * LANES + lax.broadcasted_iota(jnp.int32, (levels, LANES), 1)
        for f in range(3):
            kept = jnp.where(slot < share, totals[f], 0.0)
            out_ref[f, :, lanes] = kept.astype(jnp.bfloat16)


def exchange(send_ref, recv_ref, send_sem, recv_sem):
    along = lax.axis_size("lon")
    total = lax.axis_size("wave") * along
    me = lax.axis_index("wave") * along + lax.axis_index("lon")

    def target_of(step):
        target = lax.rem(me + step, total)
        return lax.div(target, along), lax.rem(target, along)

    def copy_at(step):
        row, place = target_of(step)
        return pltpu.make_async_remote_copy(
            src_ref=send_ref.at[row],
            dst_ref=recv_ref.at[me],
            send_sem=send_sem.at[step],
            recv_sem=recv_sem.at[step],
            device_id=(row, place),
            device_id_type=pl.DeviceIdType.MESH,
        )

    def greet():
        barrier = pltpu.get_barrier_semaphore()

        def one(step, carry):
            pl.semaphore_signal(
                barrier, inc=1, device_id=target_of(step), device_id_type=pl.DeviceIdType.MESH
            )
            return carry

        lax.fori_loop(1, total, one, 0)

    def start():
        pl.semaphore_wait(pltpu.get_barrier_semaphore(), total - 1)

        def one(step, carry):
            copy_at(step).start()
            return carry

        lax.fori_loop(1, total, one, 0)
        recv_ref[me] = send_ref[lax.axis_index("wave")]

    def finish():
        def one(step, carry):
            copy_at(step).wait()
            return carry

        lax.fori_loop(1, total, one, 0)

    return greet, start, finish


def row_kernel(
    seg_count, length_ref, own_ref, pairs_ref, spectra_ref, legendre_ref, spread_ref, order_ref,
    departure_ref, weights_ref, out_ref, rhs_ref, send_f, send_ref,
    table_ref, start_cos, start_sin, lhs_ref, grid_ref, recv_ref, fourier_ref, send_sem, recv_sem,
):
    length = length_ref[0]
    levels, width = departure_ref.shape
    blocks = width // LANES
    greet, start, finish = exchange(send_ref, recv_ref, send_sem, recv_sem)
    greet()
    pair_dev = legendre_ref.shape[0]
    legendre_sums(
        pair_dev, own_ref, spectra_ref, legendre_ref, spread_ref, send_ref, rhs_ref, send_f
    )
    start()
    make_tables(seg_count, pairs_ref, length, table_ref, start_cos, start_sin)
    finish()
    along = lax.axis_size("lon")
    waves = lax.axis_size("wave")
    for i in range(waves):
        parts = jnp.concatenate([recv_ref[i * along + g] for g in range(along)], axis=0)
        ordered = jnp.dot(order_ref[...], parts, preferred_element_type=jnp.float32)
        for s in range(2):
            at = (s * waves + i) * pair_dev
            fourier_ref[:, at : at + pair_dev] = ordered[:, s * pair_dev : (s + 1) * pair_dev]
    real = fourier_ref[: 3 * levels]
    imag = fourier_ref[3 * levels :]
    synthesize(real, imag, blocks, table_ref, start_cos, start_sin, lhs_ref, grid_ref)
    depart(length // seg_count, blocks, levels, departure_ref, weights_ref, grid_ref, out_ref)


def legendre_sums(
    pair_dev, pairs_ref, spectra_ref, legendre_ref, spread_ref, send_ref, rhs_ref, send_f
):
    columns, padded, packed = spectra_ref.shape
    row_total = legendre_ref.shape[1]
    chunk = send_ref.shape[1]
    start = lax.axis_index("wave") * pair_dev
    lane = lax.broadcasted_iota(jnp.int32, (row_total, packed), 1)
    zero = jnp.zeros((row_total, packed), jnp.float32)
    wide = 2 * GROUP * row_total
    own = lax.broadcasted_iota(jnp.int32, (GROUP, wide), 0)
    other = lax.broadcasted_iota(jnp.int32, (GROUP, wide), 1)
    low = jnp.where(other >= wide // 2, other - wide // 2, other) - own * row_total
    mine = jnp.where((low >= 0) & (low < row_total), 1.0, 0.0)[None]
    send_f[...] = jnp.zeros_like(send_f)
    for g in range(padded // GROUP):
        for p in range(0, GROUP, 2):
            first, second = [], []
            for at in (g * GROUP + p, g * GROUP + p + 1):
                if at < pair_dev:
                    rows = legendre_ref[at].astype(jnp.float32)
                    keep = lane < TRUNC + 1 - pairs_ref[start + at]
                    first.append(jnp.where(keep, rows, 0.0))
                    second.append(jnp.where(keep, 0.0, rows))
                else:
                    first.append(zero)
                    second.append(zero)
            for s, part in enumerate((first, second)):
                at = (s * GROUP + p) * row_total
                part = jnp.concatenate(part, axis=0).astype(jnp.bfloat16)
                rhs_ref[g, at : at + 2 * row_total] = part
        lhs = spectra_ref[:, g * GROUP : (g + 1) * GROUP, :].reshape(columns * GROUP, packed)
        cross = lax.dot_general(
            lhs, rhs_ref[g], (((1,), (1,)), ((), ())), preferred_element_type=jnp.float32
        )
        sums = jnp.sum(cross.reshape(columns, GROUP, wide) * mine, axis=1).astype(jnp.bfloat16)
        by_row = jnp.dot(sums, spread_ref[...], preferred_element_type=jnp.float32)
        valid = min(GROUP, pair_dev - g * GROUP)
        for j in range(row_total):
            for s in range(2):
                source = (j * 2 + s) * GROUP
                to = s * pair_dev + g * GROUP
                send_f[j, :columns, to : to + valid] = by_row[:, source : source + valid]
    for j in range(row_total):
        send_ref[j] = send_f[j].astype(jnp.bfloat16)


def lane_order(row_total):
    wide = 2 * GROUP * row_total
    source = np.arange(wide).reshape(2, GROUP, row_total).transpose(2, 0, 1).reshape(-1)
    order = np.zeros((wide, wide), np.float32)
    order[source, np.arange(wide)] = 1.0
    return jnp.asarray(order, jnp.bfloat16)


def row_order(levels, level_dev, chunk):
    order = np.zeros((6 * levels, levels // level_dev * chunk), np.float32)
    for part_field in range(6):
        for v in range(levels):
            source = v // level_dev * chunk + part_field * level_dev + v % level_dev
            order[part_field * levels + v, source] = 1.0
    return jnp.asarray(order, jnp.bfloat16)


def local(spectra, legendre, pair_waves, row_lengths, departure, weights):
    pair_dev = spectra.shape[0]
    level_dev = spectra.shape[3]
    packed = spectra.shape[4]
    row_total = legendre.shape[1]
    pairs = pair_waves.shape[0]
    levels, width = departure.shape[1], departure.shape[3]
    seg_count = lax.axis_size("lon")
    columns = 6 * level_dev
    padded = -(-pair_dev // GROUP) * GROUP
    chunk = -(-columns // 16) * 16
    flat_spec = jnp.transpose(spectra, (1, 2, 3, 0, 4)).reshape(columns, pair_dev, packed)
    flat_spec = jnp.pad(flat_spec, ((0, 0), (0, padded - pair_dev), (0, 0)))
    vmem = pl.BlockSpec(memory_space=pltpu.VMEM)
    smem = pl.BlockSpec(memory_space=pltpu.SMEM)
    wide = 2 * GROUP * row_total
    devices = lax.axis_size("wave") * seg_count
    blocks = width // LANES
    modes = 2 * pairs
    result = pl.pallas_call(
        functools.partial(row_kernel, seg_count),
        out_shape=jax.ShapeDtypeStruct((3, levels, width), jnp.bfloat16),
        in_specs=[smem] * 2 + [vmem] * 7,
        out_specs=vmem,
        scratch_shapes=[
            pltpu.VMEM((padded // GROUP, wide, packed), jnp.bfloat16),
            pltpu.VMEM((row_total, chunk, 2 * pair_dev), jnp.float32),
            pltpu.VMEM((row_total, chunk, 2 * pair_dev), jnp.bfloat16),
            pltpu.VMEM((SPAN, 2 * modes), jnp.bfloat16),
            pltpu.VMEM((16, modes), jnp.float32),
            pltpu.VMEM((16, modes), jnp.float32),
            pltpu.VMEM((blocks * 3 * levels, 2 * modes), jnp.float32),
            pltpu.VMEM((blocks * 3 * levels, 2 * LANES), jnp.float32),
            pltpu.VMEM((devices, chunk, 2 * pair_dev), jnp.bfloat16),
            pltpu.VMEM((6 * levels, modes), jnp.float32),
            pltpu.SemaphoreType.DMA((devices,)),
            pltpu.SemaphoreType.DMA((devices,)),
        ],
        compiler_params=pltpu.CompilerParams(
            vmem_limit_bytes=40 * 1024 * 1024, collective_id=0, has_side_effects=True
        ),
    )(
        row_lengths,
        pair_waves,
        pair_waves[None, :],
        flat_spec,
        legendre,
        lane_order(row_total),
        row_order(levels, level_dev, chunk),
        departure[0, :, 0, :],
        weights[:, 0, :, 0, :],
    )
    return result[:, None, :, None, :]


def solution(mesh):
    return jax.shard_map(
        local,
        mesh=mesh,
        in_specs=(
            P("wave", None, None, "lon", None),
            P("wave", None, None),
            P(),
            P("wave"),
            P("wave", None, "lon", None),
            P(None, "wave", None, "lon", None),
        ),
        out_specs=P(None, "wave", None, "lon", None),
        check_vma=False,
    )
```

```python
import functools
import math

import jax
import jax.numpy as jnp
import numpy as np
from jax import lax
from jax.experimental import pallas as pl
from jax.experimental.pallas import tpu as pltpu
from jax.sharding import PartitionSpec as P

TRUNC = 1279
HALO = 8
LANES = 128
GROUP = 16
SHIFTS = 2 * HALO + 1
SPAN = LANES + 2 * HALO


def unit_circle(waves, points, length, inverse):
    product = waves * points
    turns = jnp.floor(product * inverse + 0.5)
    half = (product - turns * length) * (inverse * math.pi)
    sq = half * half
    sine, cosine = 0.0, 0.0
    for k in range(7, -1, -1):
        sine = sine * sq + (-1.0) ** k / math.factorial(2 * k + 1)
        cosine = cosine * sq + (-1.0) ** k / math.factorial(2 * k)
    sine = sine * half
    return 1.0 - 2.0 * sine * sine, 2.0 * sine * cosine


def make_tables(seg_count, pairs_ref, length, table_ref, start_cos, start_sin):
    first = pairs_ref[...].reshape(1, -1).astype(jnp.float32)
    waves = jnp.concatenate([first, TRUNC - first], axis=1)
    modes = waves.shape[1]
    length_f = length.astype(jnp.float32)
    inverse = 1.0 / jnp.full((1, 1), length_f, jnp.float32)
    fine_at = lax.broadcasted_iota(jnp.int32, (16, modes), 0).astype(jnp.float32)
    cos_f, sin_f = unit_circle(waves, fine_at, length_f, inverse)
    cos_c, sin_c = unit_circle(waves, fine_at * 16.0, length_f, inverse)
    for a in range(SPAN // 16):
        ca, sa = cos_c[a : a + 1], sin_c[a : a + 1]
        rows = slice(16 * a, 16 * a + 16)
        table_ref[rows, :modes] = (cos_f * ca - sin_f * sa).astype(jnp.bfloat16)
        table_ref[rows, modes:] = (-(sin_f * ca + cos_f * sa)).astype(jnp.bfloat16)
    share = length // seg_count
    start = (lax.axis_index("lon") * share - HALO).astype(jnp.float32)
    cos_s, sin_s = unit_circle(waves, fine_at * float(LANES) + start, length_f, inverse)
    highest = (length // 2 - 1).astype(jnp.float32)
    factor = jnp.where(waves == 0.0, 1.0, jnp.where(waves <= highest, 2.0, 0.0))
    start_cos[...] = cos_s * factor
    start_sin[...] = sin_s * factor


def synthesize(real, imag, blocks, table_ref, start_cos, start_sin, lhs_ref, grid_ref):
    rows, modes = real.shape
    for h in range(blocks):
        c, s = start_cos[h : h + 1], start_sin[h : h + 1]
        at = slice(h * rows, (h + 1) * rows)
        lhs_ref[at, :modes] = real * c - imag * s
        lhs_ref[at, modes:] = real * s + imag * c
    grid_ref[:, :SPAN] = lax.dot_general(
        lhs_ref[...].astype(jnp.bfloat16),
        table_ref[...],
        (((1,), (1,)), ((), ())),
        preferred_element_type=jnp.float32,
    )


def depart(share, blocks, levels, departure_ref, weights_ref, grid_ref, out_ref):
    rows = 3 * levels
    for h in range(blocks):
        lanes = slice(h * LANES, (h + 1) * LANES)
        cell = departure_ref[:, lanes]
        factors = [weights_ref[c, :, lanes].astype(jnp.float32) for c in range(4)]
        totals = [jnp.zeros((levels, LANES), jnp.float32)] * 3
        for s in range(SHIFTS):
            weight = jnp.zeros((levels, LANES), jnp.float32)
            for c in range(4):
                if 1 - HALO <= s - 7 - c <= HALO - 2:
                    weight = weight + jnp.where(cell == s - 7 - c, factors[c], 0.0)
            moved = grid_ref[h * rows : (h + 1) * rows, s : s + LANES]
            for f in range(3):
                totals[f] = totals[f] + weight * moved[f * levels : (f + 1) * levels]
        slot = h * LANES + lax.broadcasted_iota(jnp.int32, (levels, LANES), 1)
        for f in range(3):
            kept = jnp.where(slot < share, totals[f], 0.0)
            out_ref[f, :, lanes] = kept.astype(jnp.bfloat16)


def exchange(send_ref, recv_ref, send_sem, recv_sem):
    along = lax.axis_size("lon")
    total = lax.axis_size("wave") * along
    me = lax.axis_index("wave") * along + lax.axis_index("lon")

    def target_of(step):
        target = lax.rem(me + step, total)
        return lax.div(target, along), lax.rem(target, along)

    def copy_at(step):
        row, place = target_of(step)
        return pltpu.make_async_remote_copy(
            src_ref=send_ref.at[row],
            dst_ref=recv_ref.at[me],
            send_sem=send_sem.at[step],
            recv_sem=recv_sem.at[step],
            device_id=(row, place),
            device_id_type=pl.DeviceIdType.MESH,
        )

    def greet():
        barrier = pltpu.get_barrier_semaphore()

        def one(step, carry):
            pl.semaphore_signal(
                barrier, inc=1, device_id=target_of(step), device_id_type=pl.DeviceIdType.MESH
            )
            return carry

        lax.fori_loop(1, total, one, 0)

    def start():
        pl.semaphore_wait(pltpu.get_barrier_semaphore(), total - 1)

        def one(step, carry):
            copy_at(step).start()
            return carry

        lax.fori_loop(1, total, one, 0)
        recv_ref[me] = send_ref[lax.axis_index("wave")]

    def finish():
        def one(step, carry):
            copy_at(step).wait()
            return carry

        lax.fori_loop(1, total, one, 0)

    return greet, start, finish


def row_kernel(
    seg_count, length_ref, own_ref, pairs_ref, spectra_ref, legendre_ref, spread_ref, order_ref,
    departure_ref, weights_ref, out_ref, rhs_ref, send_f, send_ref, cells_ref,
    table_ref, start_cos, start_sin, lhs_ref, grid_ref, recv_ref, fourier_ref, send_sem, recv_sem,
):
    length = length_ref[0]
    levels, _, width = departure_ref.shape
    blocks = width // LANES
    greet, start, finish = exchange(send_ref, recv_ref, send_sem, recv_sem)
    greet()
    pair_dev = legendre_ref.shape[0]
    legendre_sums(
        pair_dev, own_ref, spectra_ref, legendre_ref, spread_ref, send_ref, rhs_ref, send_f
    )
    start()
    make_tables(seg_count, pairs_ref, length, table_ref, start_cos, start_sin)
    for v in range(levels):
        cells_ref[v : v + 1] = departure_ref[v]
    finish()
    along = lax.axis_size("lon")
    waves = lax.axis_size("wave")
    for i in range(waves):
        parts = jnp.concatenate([recv_ref[i * along + g] for g in range(along)], axis=0)
        ordered = jnp.dot(order_ref[...], parts, preferred_element_type=jnp.float32)
        for s in range(2):
            at = (s * waves + i) * pair_dev
            fourier_ref[:, at : at + pair_dev] = ordered[:, s * pair_dev : (s + 1) * pair_dev]
    real = fourier_ref[: 3 * levels]
    imag = fourier_ref[3 * levels :]
    synthesize(real, imag, blocks, table_ref, start_cos, start_sin, lhs_ref, grid_ref)
    depart(length // seg_count, blocks, levels, cells_ref, weights_ref, grid_ref, out_ref)


def legendre_sums(
    pair_dev, pairs_ref, spectra_ref, legendre_ref, spread_ref, send_ref, rhs_ref, send_f
):
    columns, padded, packed = spectra_ref.shape
    row_total = legendre_ref.shape[1]
    chunk = send_ref.shape[1]
    start = lax.axis_index("wave") * pair_dev
    lane = lax.broadcasted_iota(jnp.int32, (row_total, packed), 1)
    zero = jnp.zeros((row_total, packed), jnp.float32)
    wide = 2 * GROUP * row_total
    own = lax.broadcasted_iota(jnp.int32, (GROUP, wide), 0)
    other = lax.broadcasted_iota(jnp.int32, (GROUP, wide), 1)
    low = jnp.where(other >= wide // 2, other - wide // 2, other) - own * row_total
    mine = jnp.where((low >= 0) & (low < row_total), 1.0, 0.0)[None]
    send_f[...] = jnp.zeros_like(send_f)
    for g in range(padded // GROUP):
        for p in range(0, GROUP, 2):
            first, second = [], []
            for at in (g * GROUP + p, g * GROUP + p + 1):
                if at < pair_dev:
                    rows = legendre_ref[at].astype(jnp.float32)
                    keep = lane < TRUNC + 1 - pairs_ref[start + at]
                    first.append(jnp.where(keep, rows, 0.0))
                    second.append(jnp.where(keep, 0.0, rows))
                else:
                    first.append(zero)
                    second.append(zero)
            for s, part in enumerate((first, second)):
                at = (s * GROUP + p) * row_total
                part = jnp.concatenate(part, axis=0).astype(jnp.bfloat16)
                rhs_ref[g, at : at + 2 * row_total] = part
        lhs = spectra_ref[:, g * GROUP : (g + 1) * GROUP, :].reshape(columns * GROUP, packed)
        cross = lax.dot_general(
            lhs, rhs_ref[g], (((1,), (1,)), ((), ())), preferred_element_type=jnp.float32
        )
        sums = jnp.sum(cross.reshape(columns, GROUP, wide) * mine, axis=1).astype(jnp.bfloat16)
        by_row = jnp.dot(sums, spread_ref[...], preferred_element_type=jnp.float32)
        valid = min(GROUP, pair_dev - g * GROUP)
        for j in range(row_total):
            for s in range(2):
                source = (j * 2 + s) * GROUP
                to = s * pair_dev + g * GROUP
                send_f[j, :columns, to : to + valid] = by_row[:, source : source + valid]
    for j in range(row_total):
        send_ref[j] = send_f[j].astype(jnp.bfloat16)


def lane_order(row_total):
    wide = 2 * GROUP * row_total
    source = np.arange(wide).reshape(2, GROUP, row_total).transpose(2, 0, 1).reshape(-1)
    order = np.zeros((wide, wide), np.float32)
    order[source, np.arange(wide)] = 1.0
    return jnp.asarray(order, jnp.bfloat16)


def row_order(levels, level_dev, chunk):
    order = np.zeros((6 * levels, levels // level_dev * chunk), np.float32)
    for part_field in range(6):
        for v in range(levels):
            source = v // level_dev * chunk + part_field * level_dev + v % level_dev
            order[part_field * levels + v, source] = 1.0
    return jnp.asarray(order, jnp.bfloat16)


def local(spectra, legendre, pair_waves, row_lengths, departure, weights):
    pair_dev = spectra.shape[0]
    level_dev = spectra.shape[3]
    packed = spectra.shape[4]
    row_total = legendre.shape[1]
    pairs = pair_waves.shape[0]
    levels, width = departure.shape[1], departure.shape[3]
    seg_count = lax.axis_size("lon")
    columns = 6 * level_dev
    padded = -(-pair_dev // GROUP) * GROUP
    chunk = -(-columns // 16) * 16
    flat_spec = jnp.transpose(spectra, (1, 2, 3, 0, 4)).reshape(columns, pair_dev, packed)
    flat_spec = jnp.pad(flat_spec, ((0, 0), (0, padded - pair_dev), (0, 0)))
    vmem = pl.BlockSpec(memory_space=pltpu.VMEM)
    smem = pl.BlockSpec(memory_space=pltpu.SMEM)
    wide = 2 * GROUP * row_total
    devices = lax.axis_size("wave") * seg_count
    blocks = width // LANES
    modes = 2 * pairs
    result = pl.pallas_call(
        functools.partial(row_kernel, seg_count),
        out_shape=jax.ShapeDtypeStruct((3, levels, width), jnp.bfloat16),
        in_specs=[smem] * 2 + [vmem] * 7,
        out_specs=vmem,
        scratch_shapes=[
            pltpu.VMEM((padded // GROUP, wide, packed), jnp.bfloat16),
            pltpu.VMEM((row_total, chunk, 2 * pair_dev), jnp.float32),
            pltpu.VMEM((row_total, chunk, 2 * pair_dev), jnp.bfloat16),
            pltpu.VMEM((levels, width), jnp.int32),
            pltpu.VMEM((SPAN, 2 * modes), jnp.bfloat16),
            pltpu.VMEM((16, modes), jnp.float32),
            pltpu.VMEM((16, modes), jnp.float32),
            pltpu.VMEM((blocks * 3 * levels, 2 * modes), jnp.float32),
            pltpu.VMEM((blocks * 3 * levels, 2 * LANES), jnp.float32),
            pltpu.VMEM((devices, chunk, 2 * pair_dev), jnp.bfloat16),
            pltpu.VMEM((6 * levels, modes), jnp.float32),
            pltpu.SemaphoreType.DMA((devices,)),
            pltpu.SemaphoreType.DMA((devices,)),
        ],
        compiler_params=pltpu.CompilerParams(
            vmem_limit_bytes=40 * 1024 * 1024, collective_id=0, has_side_effects=True
        ),
    )(
        row_lengths,
        pair_waves,
        pair_waves,
        flat_spec,
        legendre,
        lane_order(row_total),
        row_order(levels, level_dev, chunk),
        departure[0],
        weights[:, 0, :, 0, :],
    )
    return result[:, None, :, None, :]


def solution(mesh):
    return jax.shard_map(
        local,
        mesh=mesh,
        in_specs=(
            P("wave", None, None, "lon", None),
            P("wave", None, None),
            P(),
            P("wave"),
            P("wave", None, "lon", None),
            P(None, "wave", None, "lon", None),
        ),
        out_specs=P(None, "wave", None, "lon", None),
        check_vma=False,
    )
```
